512 devices in a mesh: row: 16 (over x, y), col: 32 (over z, core).
Axes of the slice: x: 4, y: 4, z: 16, core: 2. Of those that a mesh axis runs over, the one named last changes fastest.
Arguments:
- tokens: bfloat16 [512, 8192], P('col', 'row'), may hold values from -6 to 6
- out_grad: bfloat16 [512, 8192], P('col', 'row'), may hold values from -1.5 to 1.5
- w_gate: bfloat16 [8192, 26624], P('row', 'col'), may hold values from -0.0625 to 0.0625
- w_up: bfloat16 [8192, 26624], P('row', 'col'), may hold values from -0.0625 to 0.0625
- w_down: bfloat16 [26624, 8192], P('col', 'row'), may hold values from -0.0390625 to 0.0390625
Outputs:
- grad_input: bfloat16 [512, 8192], P('col', 'row')
- grad_gate_w: bfloat16 [8192, 26624], P('row', 'col')
- grad_up_w: bfloat16 [8192, 26624], P('row', 'col')
- grad_down_w: bfloat16 [26624, 8192], P('col', 'row')
The draws below stay inside these ranges and needn't reach their ends.
All inputs are finite; a program needn't handle non-finite values.
Results may differ from the reference program's by a relative error of at most 0.0049.
Values may be sent and summed in bfloat16 or wider, within the bound.
No kernel may reach another device: no remote copies, remote signals or barrier semaphores. Data moves between devices by JAX's collectives and lax.ppermute only.
A program may use at most 64 MiB of HBM per device.

```python
import jax
import jax.numpy as jnp

D = 8192
FF = 26624
TOKENS = 512


def steps_of(rng, dims, cuts, smallest, high):
    gain = 1.0
    for position, shards_of in cuts:
        heights = jax.random.uniform(jax.random.fold_in(jax.random.fold_in(rng, 6), position), (shards_of,), jnp.float32, smallest / len(cuts), high / len(cuts))
        gain = gain * jnp.repeat(jnp.exp(heights), dims[position] // shards_of).reshape((-1,) + (1,) * (len(dims) - 1 - position))
    return gain


def scatter_about(own_key, extent, spread, bound, split=(), dtype=jnp.bfloat16):
    factor_of = steps_of(own_key, extent, split, -0.22, 0.18) if split else 1.0
    array = jax.random.normal(own_key, extent, jnp.float32) * spread * factor_of
    return jnp.minimum(jnp.maximum(array, -bound), bound).astype(dtype)


def setup_inputs(seed: int = 0) -> dict:
    splits = jax.random.split(jax.random.key(seed), 6)
    tokens = scatter_about(splits[0], (TOKENS, D), 1.0, 6.0, ((0, 32), (1, 16)))
    out_grad = scatter_about(splits[1], (TOKENS, D), 0.25, 1.5, ((0, 32), (1, 16)))
    w_gate = scatter_about(splits[2], (D, FF), D ** -0.5, 0.0625, ((0, 16), (1, 32)))
    w_up = scatter_about(splits[3], (D, FF), D ** -0.5, 0.0625, ((0, 16), (1, 32)))
    w_down = scatter_about(splits[4], (FF, D), FF ** -0.5, 0.0390625, ((0, 32), (1, 16)))
    return dict(tokens=tokens, out_grad=out_grad, w_gate=w_gate, w_up=w_up, w_down=w_down)


def reference(tokens, out_grad, w_gate, w_up, w_down):
    gate = jnp.dot(tokens, w_gate, preferred_element_type=jnp.float32)
    up = jnp.dot(tokens, w_up, preferred_element_type=jnp.float32)
    back = jnp.dot(out_grad, w_down.T, preferred_element_type=jnp.float32)
    sig = jax.nn.sigmoid(gate)
    active = gate * sig
    hidden = (active * up).astype(jnp.bfloat16)
    grad_gate = (back * up * sig * (1.0 + gate * (1.0 - sig))).astype(jnp.bfloat16)
    grad_up = (back * active).astype(jnp.bfloat16)
    grad_input = (jnp.dot(grad_gate, w_gate.T, preferred_element_type=jnp.float32)
                  + jnp.dot(grad_up, w_up.T, preferred_element_type=jnp.float32)).astype(jnp.bfloat16)
    grad_gate_w = jnp.dot(tokens.T, grad_gate, preferred_element_type=jnp.float32).astype(jnp.bfloat16)
    grad_up_w = jnp.dot(tokens.T, grad_up, preferred_element_type=jnp.float32).astype(jnp.bfloat16)
    grad_down_w = jnp.dot(hidden.T, out_grad, preferred_element_type=jnp.float32).astype(jnp.bfloat16)
    return grad_input, grad_gate_w, grad_up_w, grad_down_w
```

```python
import jax
import jax.numpy as jnp
from jax import lax
from jax.sharding import Mesh, PartitionSpec as P

ROW = ("x", "y")
SWAP = [(0, 1), (1, 0)]


def swiglu_back(gate, up, back):
    sig = jax.nn.sigmoid(gate)
    active = gate * sig
    hidden = (active * up).astype(jnp.bfloat16)
    grad_gate = (back * up * sig * (1.0 + gate * (1.0 - sig))).astype(jnp.bfloat16)
    grad_up = (back * active).astype(jnp.bfloat16)
    return (hidden, grad_gate, grad_up)


def dot(spec, a, b):
    return jnp.einsum(spec, a, b, preferred_element_type=jnp.float32)


def per_device(tokens, out_grad, w_gate, w_up, w_down):
    own = lax.all_gather(jnp.concatenate([tokens, out_grad], 1), "z", axis=0, tiled=True)
    other = lax.ppermute(own, "c", SWAP)
    both = jnp.concatenate([own, other], 0)
    width, hid = w_gate.shape
    count = both.shape[0]
    all_tokens, all_grads = both[:, :width], both[:, width:]
    parts = jnp.concatenate(
        [
            dot("td,df->tf", all_tokens, w_gate).astype(jnp.bfloat16),
            dot("td,df->tf", all_tokens, w_up).astype(jnp.bfloat16),
            dot("td,fd->tf", all_grads, w_down).astype(jnp.bfloat16),
        ],
        1,
    )
    rows = lax.axis_size("x") * lax.axis_size("y")
    parts = parts.reshape(rows, count // rows, 3 * hid)
    parts = lax.all_to_all(parts, ROW, split_axis=0, concat_axis=0, tiled=True)
    total = jnp.sum(parts.astype(jnp.float32), 0)
    made = swiglu_back(total[:, :hid], total[:, hid : 2 * hid], total[:, 2 * hid :])
    made = jnp.concatenate(made, 1)
    made = jnp.broadcast_to(made[None], (rows,) + made.shape)
    made = lax.all_to_all(made, ROW, split_axis=0, concat_axis=0, tiled=True)
    made = made.reshape(count, 3 * hid)
    hidden, grad_gate, grad_up = made[:, :hid], made[:, hid : 2 * hid], made[:, 2 * hid :]
    part = dot("tf,df->td", grad_gate, w_gate) + dot("tf,df->td", grad_up, w_up)
    part = part[: count // 2] + lax.ppermute(part[count // 2 :], "c", SWAP)
    depth = lax.axis_size("z")
    part = part.astype(jnp.bfloat16).reshape(depth, count // 2 // depth, width)
    part = lax.all_to_all(part, "z", split_axis=0, concat_axis=0, tiled=True)
    grad_input = jnp.sum(part.astype(jnp.float32), 0).astype(jnp.bfloat16)
    grad_gate_w = dot("td,tf->df", all_tokens, grad_gate).astype(jnp.bfloat16)
    grad_up_w = dot("td,tf->df", all_tokens, grad_up).astype(jnp.bfloat16)
    grad_down_w = dot("tf,td->fd", hidden, all_grads).astype(jnp.bfloat16)
    return (grad_input, grad_gate_w, grad_up_w, grad_down_w)


def solution(mesh):
    mesh = Mesh(mesh.devices.reshape(4, 4, 16, 2), ("x", "y", "z", "c"))
    col = ("z", "c")
    placed = (P(col, ROW), P(col, ROW), P(ROW, col), P(ROW, col), P(col, ROW))
    return jax.shard_map(
        per_device,
        mesh=mesh,
        in_specs=placed,
        out_specs=(P(col, ROW), P(ROW, col), P(ROW, col), P(col, ROW)),
        check_vma=False,
    )
```

```python
import functools


import jax
import jax.numpy as jnp
from jax import lax
from jax.experimental import pallas as pl
from jax.experimental.pallas import tpu as pltpu
from jax.sharding import Mesh, PartitionSpec as P

ROW = ("x", "y")
SWAP = [(0, 1), (1, 0)]
B, F = jnp.bfloat16, jnp.float32
SIDE = 4
NN, NT, TN = ((1,), (0,)), ((1,), (1,)), ((0,), (0,))


def call(body, outs, *args, weights=(), scratch=()):
    many = isinstance(outs, list)
    shapes = [jax.ShapeDtypeStruct(s, d) for s, d in (outs if many else [outs])]
    made = pl.pallas_call(
        body,
        out_shape=shapes,
        in_specs=[pl.BlockSpec(memory_space=pltpu.HBM)] * len(weights)
        + [pl.BlockSpec(memory_space=pltpu.VMEM)] * len(args),
        out_specs=[pl.BlockSpec(memory_space=pltpu.VMEM)] * len(shapes),
        scratch_shapes=list(scratch),
        compiler_params=pltpu.CompilerParams(vmem_limit_bytes=24 << 20),
        cost_estimate=pl.CostEstimate(flops=1 << 30, bytes_accessed=4 << 20, transcendentals=0),
    )(*weights, *args)
    return made if many else made[0]


def mm(a, b, dims):
    return lax.dot_general(a, b, (dims, ((), ())), preferred_element_type=F)


def products(weights, tokens, store):
    hid, width = weights[0].shape
    rows, lanes = hid // SIDE, 2 * tokens.shape[0] // SIDE
    for i, w in enumerate(weights):
        part = mm(w[...], tokens[:, width:] if i == 2 else tokens[:, :width], NT).astype(B)
        for k in range(SIDE // 2):
            for j in range(SIDE):
                store(k, j, i, part[j * rows : (j + 1) * rows, k * lanes : (k + 1) * lanes])


def own_parts_kernel(wg, wu, wd, own, out, *held_and_sems):
    *held, sems = held_and_sems
    copies = [pltpu.make_async_copy(w, v, sems.at[i]) for i, (w, v) in enumerate(zip((wg, wu, wd), held))]
    for copy in copies:
        copy.start()
    for copy in copies:
        copy.wait()

    def store(k, j, i, part):
        out[k * SIDE + j, i] = part

    products(held, own, store)


def parts_kernel(other, first, wg, wu, wd, out):
    half = first.shape[0]

    def store(k, j, i, part):
        out[half + k * SIDE + j, i] = part
        out[k * SIDE + j, i] = first[k * SIDE + j, i]

    products((wg, wu, wd), other, store)


def back_kernel(got, spread, hidden):
    gate, up, back = (sum(got[r, i].astype(F) for r in range(got.shape[0])) for i in range(3))
    sig = jax.nn.sigmoid(gate)
    active = gate * sig
    hidden[...] = (active * up).astype(B)
    grad_gate = (back * up * sig * (1.0 + gate * (1.0 - sig))).astype(B)
    grad_up = (back * active).astype(B)
    for r in range(spread.shape[0]):
        spread[r, 0] = grad_gate
        spread[r, 1] = grad_up


def all_of(blocks, half=None):
    chosen = range(SIDE) if half is None else range(half * SIDE // 2, (half + 1) * SIDE // 2)
    columns = [jnp.concatenate([blocks(i, j) for j in range(SIDE)], 0) for i in chosen]
    return jnp.concatenate(columns, 1)


def input_kernel(half, grads, wg, wu, out):
    out[...] = sum(
        mm(all_of(lambda i, j: grads[i * SIDE + j, p], half), w[...], TN) for p, w in enumerate((wg, wu))
    )


def gate_up_kernel(grads, own, other, *outs):
    half, width = own.shape[0], outs[0].shape[1]
    for p, out in enumerate(outs):
        g = all_of(lambda i, j: grads[i * SIDE + j, p])
        part = mm(g[:, :half], own[:, :width], NN) + mm(g[:, half:], other[:, :width], NN)
        out[...] = part.astype(B)


def down_kernel(hidden, own, other, out):
    half, width = own.shape[0], out.shape[1]
    h = all_of(lambda i, j: hidden[i * SIDE + j])
    part = mm(h[:, :half], own[:, width:], NN) + mm(h[:, half:], other[:, width:], NN)
    out[...] = part.astype(B)


def spread_over(x, axes):
    return lax.all_to_all(x, axes, split_axis=0, concat_axis=0, tiled=True)


def per_device(tokens, out_grad, w_gate, w_up, w_down):
    hid, width = w_down.shape
    depth = lax.axis_size("z")
    own = lax.all_gather(jnp.concatenate([tokens, out_grad], 1), "z", axis=0, tiled=True)
    other = lax.ppermute(own, "c", SWAP)
    half = own.shape[0]
    rows, lanes, ranks = hid // SIDE, 2 * half // SIDE, SIDE * SIDE
    wg, wu, w_down = (pltpu.with_memory_space_constraint(w, pltpu.HBM) for w in (w_gate.T, w_up.T, w_down))

    sizes = (ranks, 3, rows, lanes)
    parts, *held = call(
        own_parts_kernel,
        [((ranks // 2,) + sizes[1:], B)] + [((hid, width), B)] * 3,
        own,
        weights=(wg, wu, w_down),
        scratch=[pltpu.SemaphoreType.DMA((3,))],
    )
    parts = call(parts_kernel, (sizes, B), other, parts, *held)
    spread, hidden = call(
        back_kernel, [((ranks, 2, rows, lanes), B), ((rows, lanes), B)], spread_over(parts, ROW)
    )
    grads = spread_over(spread, ROW)
    hidden = lax.all_gather(hidden, ROW, axis=0, tiled=False)

    rest, mine = (
        call(functools.partial(input_kernel, h), ((half, width), F), grads, *held[:2]) for h in (1, 0)
    )
    part = (mine + lax.ppermute(rest, "c", SWAP)).astype(B)
    part = spread_over(part.reshape(depth, half // depth, width), "z")
    grad_input = jnp.sum(part.astype(F), 0).astype(B)
    grad_gate_w, grad_up_w = call(gate_up_kernel, [((hid, width), B)] * 2, grads, own, other)
    grad_down_w = call(down_kernel, ((hid, width), B), hidden, own, other)
    return (grad_input, grad_gate_w.T, grad_up_w.T, grad_down_w)


def solution(mesh):
    shape = (SIDE, SIDE, mesh.devices.shape[1] // 2, 2)
    mesh = Mesh(mesh.devices.reshape(shape), ("x", "y", "z", "c"))
    col = ("z", "c")
    placed = (P(col, ROW), P(col, ROW), P(ROW, col), P(ROW, col), P(col, ROW))
    return jax.shard_map(
        per_device,
        mesh=mesh,
        in_specs=placed,
        out_specs=(P(col, ROW), P(ROW, col), P(ROW, col), P(col, ROW)),
        check_vma=False,
    )
```

```python
import functools


import jax
import jax.numpy as jnp
from jax import lax
from jax.experimental import pallas as pl
from jax.experimental.pallas import tpu as pltpu
from jax.sharding import Mesh, PartitionSpec as P

ROW = ("x", "y")
SWAP = [(0, 1), (1, 0)]
B, F = jnp.bfloat16, jnp.float32
SIDE = 4
NN, NT, TN = ((1,), (0,)), ((1,), (1,)), ((0,), (0,))


def call(body, outs, *args, weights=(), scratch=()):
    many = isinstance(outs, list)
    shapes = [jax.ShapeDtypeStruct(s, d) for s, d in (outs if many else [outs])]
    made = pl.pallas_call(
        body,
        out_shape=shapes,
        in_specs=[pl.BlockSpec(memory_space=pltpu.HBM)] * len(weights)
        + [pl.BlockSpec(memory_space=pltpu.SMEM if a.dtype == jnp.int32 else pltpu.VMEM) for a in args],
        out_specs=[pl.BlockSpec(memory_space=pltpu.VMEM)] * len(shapes),
        scratch_shapes=list(scratch),
        compiler_params=pltpu.CompilerParams(vmem_limit_bytes=24 << 20),
        cost_estimate=pl.CostEstimate(flops=1 << 30, bytes_accessed=4 << 20, transcendentals=0),
    )(*weights, *args)
    return made if many else made[0]


def mm(a, b, dims):
    return lax.dot_general(a, b, (dims, ((), ())), preferred_element_type=F)


def products(weights, tokens, store):
    hid, width = weights[0].shape
    rows, lanes = hid // SIDE, 2 * tokens.shape[0] // SIDE
    for i, w in enumerate(weights):
        part = mm(w[...], tokens[:, width:] if i == 2 else tokens[:, :width], NT).astype(B)
        for k in range(SIDE // 2):
            for j in range(SIDE):
                store(k, j, i, part[j * rows : (j + 1) * rows, k * lanes : (k + 1) * lanes])


def own_parts_kernel(wg, wu, wd, own, out, *held_and_sems):
    *held, sems = held_and_sems
    copies = [pltpu.make_async_copy(w, v, sems.at[i]) for i, (w, v) in enumerate(zip((wg, wu, wd), held))]
    for copy in copies:
        copy.start()
    for copy in copies:
        copy.wait()

    def store(k, j, i, part):
        out[k * SIDE + j, i] = part

    products(held, own, store)


def parts_kernel(other, first, wg, wu, wd, out):
    half = first.shape[0]

    def store(k, j, i, part):
        out[half + k * SIDE + j, i] = part
        out[k * SIDE + j, i] = first[k * SIDE + j, i]

    products((wg, wu, wd), other, store)


def back_kernel(got, spread, hidden):
    gate, up, back = (sum(got[r, i].astype(F) for r in range(got.shape[0])) for i in range(3))
    sig = jax.nn.sigmoid(gate)
    active = gate * sig
    hidden[...] = (active * up).astype(B)
    grad_gate = (back * up * sig * (1.0 + gate * (1.0 - sig))).astype(B)
    grad_up = (back * active).astype(B)
    for r in range(spread.shape[0]):
        spread[r, 0] = grad_gate
        spread[r, 1] = grad_up


def all_of(blocks, half=None):
    chosen = range(SIDE) if half is None else range(half * SIDE // 2, (half + 1) * SIDE // 2)
    columns = [jnp.concatenate([blocks(i, j) for j in range(SIDE)], 0) for i in chosen]
    return jnp.concatenate(columns, 1)


def input_kernel(half, grads, wg, wu, out):
    out[...] = sum(
        mm(all_of(lambda i, j: grads[i * SIDE + j, p], half), w[...], TN) for p, w in enumerate((wg, wu))
    )


def gate_up_kernel(grads, own, other, *outs):
    half, width = own.shape[0], outs[0].shape[1]
    for p, out in enumerate(outs):
        g = all_of(lambda i, j: grads[i * SIDE + j, p])
        part = mm(g[:, :half], own[:, :width], NN) + mm(g[:, half:], other[:, :width], NN)
        out[...] = part.astype(B)


def down_kernel(hidden, own, other, y, out):
    half, width = own.shape[0], out.shape[1]
    rows = out.shape[0] // SIDE
    h = all_of(lambda i, k: hidden[i * SIDE + k])
    part = mm(h[:, :half], own[:, width:], NN) + mm(h[:, half:], other[:, width:], NN)
    for k in range(SIDE):
        to = pl.ds(pl.multiple_of(lax.rem(y[0] + k, SIDE) * rows, 16), rows)
        out[to] = part[k * rows : (k + 1) * rows].astype(B)


def spread_over(x, axes):
    return lax.all_to_all(x, axes, split_axis=0, concat_axis=0, tiled=True)


def per_device(tokens, out_grad, w_gate, w_up, w_down):
    hid, width = w_down.shape
    depth = lax.axis_size("z")
    own = lax.all_gather(jnp.concatenate([tokens, out_grad], 1), "z", axis=0, tiled=True)
    other = lax.ppermute(own, "c", SWAP)
    half = own.shape[0]
    rows, lanes, ranks = hid // SIDE, 2 * half // SIDE, SIDE * SIDE
    wg, wu, w_down = (pltpu.with_memory_space_constraint(w, pltpu.HBM) for w in (w_gate.T, w_up.T, w_down))

    sizes = (ranks, 3, rows, lanes)
    parts, *held = call(
        own_parts_kernel,
        [((ranks // 2,) + sizes[1:], B)] + [((hid, width), B)] * 3,
        own,
        weights=(wg, wu, w_down),
        scratch=[pltpu.SemaphoreType.DMA((3,))],
    )
    parts = call(parts_kernel, (sizes, B), other, parts, *held)
    spread, hidden = call(
        back_kernel, [((ranks, 2, rows, lanes), B), ((rows, lanes), B)], spread_over(parts, ROW)
    )
    grads = spread_over(spread, ROW)
    turns = ([(i, (i - k) % SIDE) for i in range(SIDE)] for k in (1, 2, 3))
    hidden = [hidden] + [lax.ppermute(hidden, "y", t) for t in turns]
    grads, hidden = lax.optimization_barrier((grads, hidden))

    rest, mine = (
        call(functools.partial(input_kernel, h), ((half, width), F), grads, *held[:2]) for h in (1, 0)
    )
    part = (mine + lax.ppermute(rest, "c", SWAP)).astype(B)
    part, hidden = lax.optimization_barrier((part.reshape(depth, half // depth, width), jnp.stack(hidden)))
    part = spread_over(part, "z")
    hidden = lax.all_gather(hidden, "x", axis=0, tiled=True)
    grad_input = jnp.sum(part.astype(F), 0).astype(B)
    grad_gate_w, grad_up_w = call(gate_up_kernel, [((hid, width), B)] * 2, grads, own, other)
    grad_down_w = call(down_kernel, ((hid, width), B), hidden, own, other, lax.axis_index("y").reshape(1))
    return (grad_input, grad_gate_w.T, grad_up_w.T, grad_down_w)


def solution(mesh):
    shape = (SIDE, SIDE, mesh.devices.shape[1] // 2, 2)
    mesh = Mesh(mesh.devices.reshape(shape), ("x", "y", "z", "c"))
    col = ("z", "c")
    placed = (P(col, ROW), P(col, ROW), P(ROW, col), P(ROW, col), P(col, ROW))
    return jax.shard_map(
        per_device,
        mesh=mesh,
        in_specs=placed,
        out_specs=(P(col, ROW), P(ROW, col), P(ROW, col), P(col, ROW)),
        check_vma=False,
    )
```

```python
import jax
import jax.numpy as jnp
from jax import lax
from jax.experimental import pallas as pl
from jax.experimental.pallas import tpu as pltpu
from jax.sharding import Mesh, PartitionSpec as P

ROW = ("x", "y")
SWAP = [(0, 1), (1, 0)]
B, F = jnp.bfloat16, jnp.float32
SIDE = 4
NN, NT, TN = ((1,), (0,)), ((1,), (1,)), ((0,), (0,))


def call(body, outs, *args, weights=(), scratch=(), cost=1 << 30):
    many = isinstance(outs, list)
    shapes = [jax.ShapeDtypeStruct(s, d) for s, d in (outs if many else [outs])]
    made = pl.pallas_call(
        body,
        out_shape=shapes,
        in_specs=[pl.BlockSpec(memory_space=pltpu.HBM)] * len(weights)
        + [pl.BlockSpec(memory_space=pltpu.SMEM if a.dtype == jnp.int32 else pltpu.VMEM) for a in args],
        out_specs=[pl.BlockSpec(memory_space=pltpu.VMEM)] * len(shapes),
        scratch_shapes=list(scratch),
        compiler_params=pltpu.CompilerParams(vmem_limit_bytes=24 << 20),
        cost_estimate=pl.CostEstimate(flops=cost, bytes_accessed=cost >> 8, transcendentals=0),
    )(*weights, *args)
    return made if many else made[0]


def mm(a, b, dims):
    return lax.dot_general(a, b, (dims, ((), ())), preferred_element_type=F)


def load_kernel(*refs):
    *weights, held, sems = refs
    copies = [pltpu.make_async_copy(w, held.at[i], sems.at[i]) for i, w in enumerate(weights)]
    for copy in copies:
        copy.start()
    for copy in copies:
        copy.wait()


def parts_kernel(own, held, away, out):
    width, rows, lanes = held.shape[2], out.shape[2], out.shape[3]
    for h, weights in enumerate((held, away)):
        for p in range(3):
            t = own[:, width:] if p == 2 else own[:, :width]
            part = mm(weights[p], t, NT).astype(B)
            for i in range(2):
                for j in range(SIDE):
                    out[(2 * h + i) * SIDE + j, p] = part[j * rows : (j + 1) * rows, i * lanes : (i + 1) * lanes]


def back_kernel(got, spread):
    gate, up, back = (sum(got[r, i].astype(F) for r in range(got.shape[0])) for i in range(3))
    sig = jax.nn.sigmoid(gate)
    active = gate * sig
    hidden = (active * up).astype(B)
    grad_gate = (back * up * sig * (1.0 + gate * (1.0 - sig))).astype(B)
    grad_up = (back * active).astype(B)
    for r in range(spread.shape[0]):
        spread[r, 0] = grad_gate
        spread[r, 1] = grad_up
        spread[r, 2] = hidden


def all_of(blocks):
    return jnp.concatenate([jnp.concatenate([blocks(i, j) for j in range(SIDE)], 0) for i in range(2)], 1)


def input_kernel(grads, held, away, out):
    out[...] = sum(
        mm(all_of(lambda i, j: grads[(2 * h + i) * SIDE + j, p]), weights[p], TN)
        for h, weights in enumerate((held, away))
        for p in range(2)
    ).astype(B)


def send_kernel(grads, out):
    out[...] = grads[out.shape[0] :]


def products_of(grads, tokens):
    width = tokens.shape[1] // 2
    for p in range(3):
        cut = slice(width, None) if p == 2 else slice(None, width)
        yield mm(all_of(lambda i, j: grads[i * SIDE + j, p]), tokens[:, cut], NN)


def own_weight_kernel(grads, own, out):
    for p, part in enumerate(products_of(grads, own)):
        out[p] = part


def weight_kernel(first, got, other, *outs):
    for p, part in enumerate(products_of(got, other)):
        outs[p][...] = (first[p] + part).astype(B)


def spread_over(x, axes):
    return lax.all_to_all(x, axes, split_axis=0, concat_axis=0, tiled=True)


def swapped(x):
    return lax.ppermute(x, "c", SWAP)


def per_device(tokens, out_grad, w_gate, w_up, w_down):
    hid, width = w_down.shape
    depth = lax.axis_size("z")
    weights = [pltpu.with_memory_space_constraint(w, pltpu.HBM) for w in (w_gate.T, w_up.T, w_down)]
    held = call(load_kernel, ((3, hid, width), B), weights=weights, scratch=[pltpu.SemaphoreType.DMA((3,))])
    away = swapped(held)
    mine, held = lax.optimization_barrier((jnp.concatenate([tokens, out_grad], 1), held))
    own = lax.all_gather(mine, "z", axis=0, tiled=True)
    half = own.shape[0]
    rows, lanes, ranks = hid // SIDE, half // 2, SIDE * SIDE

    sizes = (ranks, 3, rows, lanes)
    parts = call(parts_kernel, (sizes, B), own, held, away)
    spread = call(back_kernel, (sizes, B), spread_over(parts, ROW))
    grads = spread_over(spread, ROW)

    part = call(input_kernel, ((half, width), B), grads, held, away)
    part, grads, own = lax.optimization_barrier((part.reshape(depth, half // depth, width), grads, own))
    part = spread_over(part, "z")
    got = swapped(call(send_kernel, ((ranks // 2,) + sizes[1:], B), grads, cost=256))
    other = swapped(own)
    first = call(own_weight_kernel, ((3, hid, width), F), grads, own, cost=1 << 35)
    grad_gate_w, grad_up_w, grad_down_w = call(
        weight_kernel, [((hid, width), B)] * 3, first, got, other, cost=256
    )
    part, grad_gate_w, grad_up_w, grad_down_w = lax.optimization_barrier(
        (part, grad_gate_w, grad_up_w, grad_down_w)
    )
    grad_input = jnp.sum(part.astype(F), 0).astype(B)
    return (grad_input, grad_gate_w.T, grad_up_w.T, grad_down_w)


def solution(mesh):
    shape = (SIDE, SIDE, mesh.devices.shape[1] // 2, 2)
    mesh = Mesh(mesh.devices.reshape(shape), ("x", "y", "z", "c"))
    col = ("z", "c")
    placed = (P(col, ROW), P(col, ROW), P(ROW, col), P(ROW, col), P(col, ROW))
    return jax.shard_map(
        per_device,
        mesh=mesh,
        in_specs=placed,
        out_specs=(P(col, ROW), P(ROW, col), P(ROW, col), P(col, ROW)),
        check_vma=False,
    )
```

```python
import functools


import jax
import jax.numpy as jnp
import numpy as np
from jax import lax
from jax.experimental import pallas as pl
from jax.experimental.pallas import tpu as pltpu
from jax.sharding import Mesh, PartitionSpec as P

ROW = ("x", "y")
ALL = ("x", "y", "z", "c")
SWAP = [(0, 1), (1, 0)]
B, F = jnp.bfloat16, jnp.float32
SIDE = 4
NN, NT, TN = ((1,), (0,)), ((1,), (1,)), ((0,), (0,))


def call(body, outs, *args, weights=(), scratch=(), cost=1 << 30):
    many = isinstance(outs, list)
    shapes = [jax.ShapeDtypeStruct(s, d) for s, d in (outs if many else [outs])]
    made = pl.pallas_call(
        body,
        out_shape=shapes,
        in_specs=[pl.BlockSpec(memory_space=pltpu.HBM)] * len(weights)
        + [pl.BlockSpec(memory_space=pltpu.SMEM if a.dtype == jnp.int32 else pltpu.VMEM) for a in args],
        out_specs=[pl.BlockSpec(memory_space=pltpu.VMEM)] * len(shapes),
        scratch_shapes=list(scratch),
        compiler_params=pltpu.CompilerParams(vmem_limit_bytes=24 << 20),
        cost_estimate=pl.CostEstimate(flops=cost, bytes_accessed=cost >> 8, transcendentals=0),
    )(*weights, *args)
    return made if many else made[0]


def mm(a, b, dims):
    return lax.dot_general(a, b, (dims, ((), ())), preferred_element_type=F)


def load_kernel(*refs):
    *weights, held, sems = refs
    copies = [pltpu.make_async_copy(w, held.at[i], sems.at[i]) for i, w in enumerate(weights)]
    for copy in copies:
        copy.start()
    for copy in copies:
        copy.wait()


def parts_kernel(own, held, away, out):
    width, rows, lanes = held.shape[2], out.shape[2], out.shape[3]
    for h, weights in enumerate((held, away)):
        for p in range(3):
            t = own[:, width:] if p == 2 else own[:, :width]
            part = mm(weights[p], t, NT).astype(B)
            for i in range(2):
                for j in range(SIDE):
                    out[(2 * h + i) * SIDE + j, p] = part[j * rows : (j + 1) * rows, i * lanes : (i + 1) * lanes]


def back_kernel(got, spread):
    gate, up, back = (sum(got[r, i].astype(F) for r in range(got.shape[0])) for i in range(3))
    sig = jax.nn.sigmoid(gate)
    active = gate * sig
    hidden = (active * up).astype(B)
    grad_gate = (back * up * sig * (1.0 + gate * (1.0 - sig))).astype(B)
    grad_up = (back * active).astype(B)
    for r in range(spread.shape[0]):
        spread[r, 0] = grad_gate
        spread[r, 1] = grad_up
        spread[r, 2] = hidden


def all_of(blocks):
    return jnp.concatenate([jnp.concatenate([blocks(i, j) for j in range(SIDE)], 0) for i in range(2)], 1)


def input_kernel(grads, held, away, out):
    out[...] = sum(
        mm(all_of(lambda i, j: grads[(2 * h + i) * SIDE + j, p]), weights[p], TN)
        for h, weights in enumerate((held, away))
        for p in range(2)
    ).astype(B)


def send_kernel(grads, out):
    out[...] = grads[out.shape[0] :]


def products_of(grads, tokens):
    width = tokens.shape[1] // 2
    for p in range(3):
        cut = slice(width, None) if p == 2 else slice(None, width)
        yield mm(all_of(lambda i, j: grads[i * SIDE + j, p]), tokens[:, cut], NN)


def own_weight_kernel(grads, own, out):
    for p, part in enumerate(products_of(grads, own)):
        out[p] = part


def weight_kernel(first, got, other, *outs):
    for p, part in enumerate(products_of(got, other)):
        outs[p][...] = (first[p] + part).astype(B)


def spread_over(x, axes):
    return lax.all_to_all(x, axes, split_axis=0, concat_axis=0, tiled=True)


PATH = [(0, 0), (0, 1), (0, 2), (0, 3), (1, 3), (1, 2), (1, 1), (2, 1)]
PATH += [(2, 2), (2, 3), (3, 3), (3, 2), (3, 1), (3, 0), (2, 0), (1, 0)]


def rows_of(shape):
    ids = np.arange(int(np.prod(shape))).reshape(shape)
    return [[int(ids[x, y, z, c]) for x, y in PATH] for z in range(shape[2]) for c in range(2)]


def over_rows(v, shape):
    return lax.all_to_all(v, ALL, split_axis=0, concat_axis=0, tiled=True, axis_index_groups=rows_of(shape))


def swapped(x):
    return lax.ppermute(x, "c", SWAP)


def per_device(shape, tokens, out_grad, w_gate, w_up, w_down):
    hid, width = w_down.shape
    depth = lax.axis_size("z")
    weights = [pltpu.with_memory_space_constraint(w, pltpu.HBM) for w in (w_gate.T, w_up.T, w_down)]
    held = call(load_kernel, ((3, hid, width), B), weights=weights, scratch=[pltpu.SemaphoreType.DMA((3,))])
    away = swapped(held)
    mine, held = lax.optimization_barrier((jnp.concatenate([tokens, out_grad], 1), held))
    own = lax.all_gather(mine, "z", axis=0, tiled=True)
    half = own.shape[0]
    rows, lanes, ranks = hid // SIDE, half // 2, SIDE * SIDE

    sizes = (ranks, 3, rows, lanes)
    parts = call(parts_kernel, (sizes, B), own, held, away)
    spread = call(back_kernel, (sizes, B), over_rows(parts, shape))
    grads = over_rows(spread, shape)

    part = call(input_kernel, ((half, width), B), grads, held, away)
    part, grads, own = lax.optimization_barrier((part.reshape(depth, half // depth, width), grads, own))
    part = spread_over(part, "z")
    got = swapped(call(send_kernel, ((ranks // 2,) + sizes[1:], B), grads, cost=256))
    other = swapped(own)
    first = call(own_weight_kernel, ((3, hid, width), F), grads, own, cost=1 << 35)
    grad_gate_w, grad_up_w, grad_down_w = call(
        weight_kernel, [((hid, width), B)] * 3, first, got, other, cost=256
    )
    part, grad_gate_w, grad_up_w, grad_down_w = lax.optimization_barrier(
        (part, grad_gate_w, grad_up_w, grad_down_w)
    )
    grad_input = jnp.sum(part.astype(F), 0).astype(B)
    return (grad_input, grad_gate_w.T, grad_up_w.T, grad_down_w)


def solution(mesh):
    shape = (SIDE, SIDE, mesh.devices.shape[1] // 2, 2)
    mesh = Mesh(mesh.devices.reshape(shape), ALL)
    col = ("z", "c")
    placed = (P(col, ROW), P(col, ROW), P(ROW, col), P(ROW, col), P(col, ROW))
    return jax.shard_map(
        functools.partial(per_device, shape),
        mesh=mesh,
        in_specs=placed,
        out_specs=(P(col, ROW), P(ROW, col), P(ROW, col), P(col, ROW)),
        check_vma=False,
    )
```

```python
import functools


import jax
import jax.numpy as jnp
import numpy as np
from jax import lax
from jax.experimental import pallas as pl
from jax.experimental.pallas import tpu as pltpu
from jax.sharding import Mesh, PartitionSpec as P

ROW = ("x", "y")
ALL = ("x", "y", "z", "c")
SWAP = [(0, 1), (1, 0)]
B, F = jnp.bfloat16, jnp.float32
SIDE = 4
NN, NT, TN = ((1,), (0,)), ((1,), (1,)), ((0,), (0,))


def call(body, outs, *args, weights=(), scratch=(), cost=1 << 30):
    many = isinstance(outs, list)
    shapes = [jax.ShapeDtypeStruct(s, d) for s, d in (outs if many else [outs])]
    made = pl.pallas_call(
        body,
        out_shape=shapes,
        in_specs=[pl.BlockSpec(memory_space=pltpu.HBM)] * len(weights)
        + [pl.BlockSpec(memory_space=pltpu.SMEM if a.dtype == jnp.int32 else pltpu.VMEM) for a in args],
        out_specs=[pl.BlockSpec(memory_space=pltpu.VMEM)] * len(shapes),
        scratch_shapes=list(scratch),
        compiler_params=pltpu.CompilerParams(vmem_limit_bytes=24 << 20),
        cost_estimate=pl.CostEstimate(flops=cost, bytes_accessed=cost >> 8, transcendentals=0),
    )(*weights, *args)
    return made if many else made[0]


def mm(a, b, dims):
    return lax.dot_general(a, b, (dims, ((), ())), preferred_element_type=F)


def load_kernel(*refs):
    *weights, held, sems = refs
    copies = [pltpu.make_async_copy(w, held.at[i], sems.at[i]) for i, w in enumerate(weights)]
    for copy in copies:
        copy.start()
    for copy in copies:
        copy.wait()


def main_of(hid):
    return hid // 128 * 128


def pieces(held, away, p):
    main = main_of(held.shape[1])
    return held[p, :main], away[p, :main], jnp.concatenate([held[p, main:], away[p, main:]], 0)


def parts_kernel(own, held, away, out):
    width, rows = held.shape[2], out.shape[2]
    for p in range(3):
        t = own[:, width:] if p == 2 else own[:, :width]
        start = 0
        for w in pieces(held, away, p):
            part = mm(t, w, NT).astype(B)
            for r in range(out.shape[0]):
                out[r, p, :, start : start + w.shape[0]] = part[r * rows : (r + 1) * rows]
            start += w.shape[0]


def back_kernel(got, spread):
    gate, up, back = (sum(got[r, i].astype(F) for r in range(got.shape[0])) for i in range(3))
    sig = jax.nn.sigmoid(gate)
    active = gate * sig
    hidden = (active * up).astype(B)
    grad_gate = (back * up * sig * (1.0 + gate * (1.0 - sig))).astype(B)
    grad_up = (back * active).astype(B)
    for r in range(spread.shape[0]):
        spread[r, 0] = grad_gate
        spread[r, 1] = grad_up
        spread[r, 2] = hidden


def plane(grads, p):
    ranks, _, rows, hid = grads.shape
    return grads[:, p].reshape(ranks * rows, hid)


def input_kernel(grads, held, away, out):
    g = jnp.concatenate([plane(grads, 0), plane(grads, 1)], 1)
    w = jnp.concatenate([piece for p in range(2) for piece in pieces(held, away, p)], 0)
    out[...] = mm(g, w, NN).astype(B)


def send_kernel(grads, own, out):
    cut = (out.shape[1] - own.shape[1]) // 3
    for p in range(3):
        out[:, p * cut : (p + 1) * cut] = plane(grads, p)[:, cut - 128 :]
    out[:, 3 * cut :] = own[...]


def own_weight_kernel(grads, own, out):
    hid, width = out.shape[1:]
    main = main_of(hid)
    for p in range(3):
        t = own[:, width:] if p == 2 else own[:, :width]
        g = plane(grads, p)
        out[p, :main] = mm(g[:, :main], t, TN)
        out[p, main:] = mm(g[:, 2 * main :], t, TN)[: hid - main]


def weight_kernel(first, got, *outs):
    hid, width = first.shape[1:]
    main = main_of(hid)
    cut = main + 128
    other = 3 * cut
    for p, out in enumerate(outs):
        t = got[:, other + width :] if p == 2 else got[:, other : other + width]
        g = got[:, p * cut : (p + 1) * cut]
        out[:main] = (first[p, :main] + mm(g[:, :main], t, TN)).astype(B)
        out[main:] = (first[p, main:] + mm(g[:, main:], t, TN)[hid - main :]).astype(B)


def spread_over(x, axes):
    return lax.all_to_all(x, axes, split_axis=0, concat_axis=0, tiled=True)


PATH = [(0, 0), (0, 1), (0, 2), (0, 3), (1, 3), (1, 2), (1, 1), (2, 1)]
PATH += [(2, 2), (2, 3), (3, 3), (3, 2), (3, 1), (3, 0), (2, 0), (1, 0)]


def rows_of(shape):
    ids = np.arange(int(np.prod(shape))).reshape(shape)
    return [[int(ids[x, y, z, c]) for x, y in PATH] for z in range(shape[2]) for c in range(2)]


def over_rows(v, shape):
    return lax.all_to_all(v, ALL, split_axis=0, concat_axis=0, tiled=True, axis_index_groups=rows_of(shape))


def swapped(x):
    return lax.ppermute(x, "c", SWAP)


def per_device(shape, tokens, out_grad, w_gate, w_up, w_down):
    hid, width = w_down.shape
    depth = lax.axis_size("z")
    weights = [pltpu.with_memory_space_constraint(w, pltpu.HBM) for w in (w_gate.T, w_up.T, w_down)]
    held = call(load_kernel, ((3, hid, width), B), weights=weights, scratch=[pltpu.SemaphoreType.DMA((3,))])
    away = swapped(held)
    mine, held = lax.optimization_barrier((jnp.concatenate([tokens, out_grad], 1), held))
    own = lax.all_gather(mine, "z", axis=0, tiled=True)
    half = own.shape[0]
    ranks = SIDE * SIDE

    sizes = (ranks, 3, half // ranks, 2 * hid)
    parts = call(parts_kernel, (sizes, B), own, held, away)
    spread = call(back_kernel, (sizes, B), over_rows(parts, shape))
    grads = over_rows(spread, shape)

    part = call(input_kernel, ((half, width), B), grads, held, away)
    part, grads, own = lax.optimization_barrier((part.reshape(depth, half // depth, width), grads, own))
    part = spread_over(part, "z")
    got = swapped(call(send_kernel, ((half, 3 * (main_of(hid) + 128) + 2 * width), B), grads, own, cost=256))
    first = call(own_weight_kernel, ((3, hid, width), F), grads, own, cost=1 << 35)
    grad_gate_w, grad_up_w, grad_down_w = call(
        weight_kernel, [((hid, width), B)] * 3, first, got, cost=256
    )
    part, grad_gate_w, grad_up_w, grad_down_w = lax.optimization_barrier(
        (part, grad_gate_w, grad_up_w, grad_down_w)
    )
    grad_input = jnp.sum(part.astype(F), 0).astype(B)
    return (grad_input, grad_gate_w.T, grad_up_w.T, grad_down_w)


def solution(mesh):
    shape = (SIDE, SIDE, mesh.devices.shape[1] // 2, 2)
    mesh = Mesh(mesh.devices.reshape(shape), ALL)
    col = ("z", "c")
    placed = (P(col, ROW), P(col, ROW), P(ROW, col), P(ROW, col), P(col, ROW))
    return jax.shard_map(
        functools.partial(per_device, shape),
        mesh=mesh,
        in_specs=placed,
        out_specs=(P(col, ROW), P(ROW, col), P(ROW, col), P(col, ROW)),
        check_vma=False,
    )
```

```python
import functools


import jax
import jax.numpy as jnp
import numpy as np
from jax import lax
from jax.experimental import pallas as pl
from jax.experimental.pallas import tpu as pltpu
from jax.sharding import Mesh, PartitionSpec as P

ROW = ("x", "y")
ALL = ("x", "y", "z", "c")
SWAP = [(0, 1), (1, 0)]
B, F = jnp.bfloat16, jnp.float32
SIDE = 4
NN, NT, TN = ((1,), (0,)), ((1,), (1,)), ((0,), (0,))


def call(body, outs, *args, weights=(), scratch=(), cost=1 << 30):
    many = isinstance(outs, list)
    shapes = [jax.ShapeDtypeStruct(s, d) for s, d in (outs if many else [outs])]
    made = pl.pallas_call(
        body,
        out_shape=shapes,
        in_specs=[pl.BlockSpec(memory_space=pltpu.HBM)] * len(weights)
        + [pl.BlockSpec(memory_space=pltpu.SMEM if a.dtype == jnp.int32 else pltpu.VMEM) for a in args],
        out_specs=[pl.BlockSpec(memory_space=pltpu.VMEM)] * len(shapes),
        scratch_shapes=list(scratch),
        compiler_params=pltpu.CompilerParams(vmem_limit_bytes=24 << 20),
        cost_estimate=pl.CostEstimate(flops=cost, bytes_accessed=cost >> 8, transcendentals=0),
    )(*weights, *args)
    return made if many else made[0]


def mm(a, b, dims):
    return lax.dot_general(a, b, (dims, ((), ())), preferred_element_type=F)


def load_kernel(*refs):
    *weights, tokens, out_grad, held, mine, sems = refs
    width = tokens.shape[1]
    pairs = [(w, held.at[i]) for i, w in enumerate(weights)]
    pairs += [(tokens, mine.at[:, pl.ds(0, width)]), (out_grad, mine.at[:, pl.ds(width, width)])]
    copies = [pltpu.make_async_copy(a, b, sems.at[i]) for i, (a, b) in enumerate(pairs)]
    for copy in copies:
        copy.start()
    for copy in copies:
        copy.wait()


def main_of(hid):
    return hid // 128 * 128


def pieces(held, away, p):
    main = main_of(held.shape[1])
    return held[p, :main], away[p, :main], jnp.concatenate([held[p, main:], away[p, main:]], 0)


def parts_kernel(own, held, away, out):
    width, rows = held.shape[2], out.shape[2]
    main = main_of(held.shape[1])

    def store(part, p, start):
        for r in range(out.shape[0]):
            out[r, p, :, start : start + part.shape[1]] = part[r * rows : (r + 1) * rows]

    rests = []
    for p in range(3):
        t = own[:, width:] if p == 2 else own[:, :width]
        first, second, rest = pieces(held, away, p)
        store(mm(t, first, NT).astype(B), p, 0)
        store(mm(t, second, NT).astype(B), p, main)
        rests.append(rest)
    cut = rests[0].shape[0]
    part = mm(own[:, :width], jnp.concatenate(rests[:2], 0), NT).astype(B)
    store(part[:, :cut], 0, 2 * main)
    store(part[:, cut:], 1, 2 * main)
    store(mm(own[:, width:], rests[2], NT).astype(B), 2, 2 * main)


def back_kernel(got, spread):
    gate, up, back = (sum(got[r, i].astype(F) for r in range(got.shape[0])) for i in range(3))
    sig = jax.nn.sigmoid(gate)
    active = gate * sig
    hidden = (active * up).astype(B)
    grad_gate = (back * up * sig * (1.0 + gate * (1.0 - sig))).astype(B)
    grad_up = (back * active).astype(B)
    for r in range(spread.shape[0]):
        spread[r, 0] = grad_gate
        spread[r, 1] = grad_up
        spread[r, 2] = hidden


def plane(grads, p):
    ranks, _, rows, hid = grads.shape
    return grads[:, p].reshape(ranks * rows, hid)


def input_kernel(grads, held, away, out):
    g = jnp.concatenate([plane(grads, 0), plane(grads, 1)], 1)
    w = jnp.concatenate([piece for p in range(2) for piece in pieces(held, away, p)], 0)
    out[...] = mm(g, w, NN).astype(B)


def send_kernel(grads, own, out):
    cut = (out.shape[1] - own.shape[1]) // 3
    for p in range(3):
        out[:, p * cut : (p + 1) * cut] = plane(grads, p)[:, cut - 128 :]
    out[:, 3 * cut :] = own[...]


def own_weight_kernel(grads, own, out):
    hid, width = out.shape[1:]
    main = main_of(hid)
    for p in range(3):
        t = own[:, width:] if p == 2 else own[:, :width]
        g = plane(grads, p)
        out[p, :main] = mm(g[:, :main], t, TN)
        out[p, main:] = mm(g[:, 2 * main :], t, TN)[: hid - main]


def weight_kernel(first, got, *outs):
    hid, width = first.shape[1:]
    main = main_of(hid)
    cut = main + 128
    other = 3 * cut
    for p, out in enumerate(outs):
        t = got[:, other + width :] if p == 2 else got[:, other : other + width]
        g = got[:, p * cut : (p + 1) * cut]
        out[:main] = (first[p, :main] + mm(g[:, :main], t, TN)).astype(B)
        out[main:] = (first[p, main:] + mm(g[:, main:], t, TN)[hid - main :]).astype(B)


def spread_over(x, axes):
    return lax.all_to_all(x, axes, split_axis=0, concat_axis=0, tiled=True)


PATH = [(0, 0), (0, 1), (0, 2), (0, 3), (1, 3), (1, 2), (1, 1), (2, 1)]
PATH += [(2, 2), (2, 3), (3, 3), (3, 2), (3, 1), (3, 0), (2, 0), (1, 0)]


def rows_of(shape):
    ids = np.arange(int(np.prod(shape))).reshape(shape)
    return [[int(ids[x, y, z, c]) for x, y in PATH] for z in range(shape[2]) for c in range(2)]


def over_rows(v, shape):
    return lax.all_to_all(v, ALL, split_axis=0, concat_axis=0, tiled=True, axis_index_groups=rows_of(shape))


def swapped(x):
    return lax.ppermute(x, "c", SWAP)


def per_device(shape, tokens, out_grad, w_gate, w_up, w_down):
    hid, width = w_down.shape
    depth = lax.axis_size("z")
    weights = [pltpu.with_memory_space_constraint(w, pltpu.HBM) for w in (w_gate.T, w_up.T, w_down)]
    held, mine = call(
        load_kernel,
        [((3, hid, width), B), ((tokens.shape[0], 2 * width), B)],
        weights=weights + [pltpu.with_memory_space_constraint(v, pltpu.HBM) for v in (tokens, out_grad)],
        scratch=[pltpu.SemaphoreType.DMA((5,))],
    )
    away = swapped(held)
    own = lax.all_gather(mine, "z", axis=0, tiled=True)
    half = own.shape[0]
    ranks = SIDE * SIDE

    sizes = (ranks, 3, half // ranks, 2 * hid)
    parts = call(parts_kernel, (sizes, B), own, held, away)
    spread = call(back_kernel, (sizes, B), over_rows(parts, shape))
    grads = over_rows(spread, shape)

    part = call(input_kernel, ((half, width), B), grads, held, away)
    part, grads, own = lax.optimization_barrier((part.reshape(depth, half // depth, width), grads, own))
    part = spread_over(part, "z")
    got = swapped(call(send_kernel, ((half, 3 * (main_of(hid) + 128) + 2 * width), B), grads, own, cost=256))
    first = call(own_weight_kernel, ((3, hid, width), F), grads, own, cost=1 << 35)
    grad_gate_w, grad_up_w, grad_down_w = call(
        weight_kernel, [((hid, width), B)] * 3, first, got, cost=256
    )
    part, grad_gate_w, grad_up_w, grad_down_w = lax.optimization_barrier(
        (part, grad_gate_w, grad_up_w, grad_down_w)
    )
    grad_input = jnp.sum(part.astype(F), 0).astype(B)
    return (grad_input, grad_gate_w.T, grad_up_w.T, grad_down_w)


def solution(mesh):
    shape = (SIDE, SIDE, mesh.devices.shape[1] // 2, 2)
    mesh = Mesh(mesh.devices.reshape(shape), ALL)
    col = ("z", "c")
    placed = (P(col, ROW), P(col, ROW), P(ROW, col), P(ROW, col), P(col, ROW))
    return jax.shard_map(
        functools.partial(per_device, shape),
        mesh=mesh,
        in_specs=placed,
        out_specs=(P(col, ROW), P(ROW, col), P(ROW, col), P(col, ROW)),
        check_vma=False,
    )
```

```python
import functools


import jax
import jax.numpy as jnp
import numpy as np
from jax import lax
from jax.experimental import pallas as pl
from jax.experimental.pallas import tpu as pltpu
from jax.sharding import Mesh, PartitionSpec as P

ROW = ("x", "y")
ALL = ("x", "y", "z", "c")
SWAP = [(0, 1), (1, 0)]
B, F = jnp.bfloat16, jnp.float32
SIDE = 4
NN, NT, TN = ((1,), (0,)), ((1,), (1,)), ((0,), (0,))


def call(body, outs, *args, weights=(), scratch=(), cost=1 << 30):
    many = isinstance(outs, list)
    shapes = [jax.ShapeDtypeStruct(s, d) for s, d in (outs if many else [outs])]
    made = pl.pallas_call(
        body,
        out_shape=shapes,
        in_specs=[pl.BlockSpec(memory_space=pltpu.HBM)] * len(weights)
        + [pl.BlockSpec(memory_space=pltpu.SMEM if a.dtype == jnp.int32 else pltpu.VMEM) for a in args],
        out_specs=[pl.BlockSpec(memory_space=pltpu.VMEM)] * len(shapes),
        scratch_shapes=list(scratch),
        compiler_params=pltpu.CompilerParams(vmem_limit_bytes=24 << 20),
        cost_estimate=pl.CostEstimate(flops=cost, bytes_accessed=cost >> 8, transcendentals=0),
    )(*weights, *args)
    return made if many else made[0]


def mm(a, b, dims):
    return lax.dot_general(a, b, (dims, ((), ())), preferred_element_type=F)


def load_kernel(*refs):
    *weights, held, sems = refs
    copies = [pltpu.make_async_copy(w, held.at[i], sems.at[i]) for i, w in enumerate(weights)]
    for copy in copies:
        copy.start()
    for copy in copies:
        copy.wait()


def main_of(hid):
    return hid // 128 * 128


def pieces(held, away, p):
    main = main_of(held.shape[1])
    return held[p, :main], away[p, :main], jnp.concatenate([held[p, main:], away[p, main:]], 0)


def parts_kernel(own, held, away, out):
    width, rows = held.shape[2], out.shape[2]
    main = main_of(held.shape[1])

    def store(part, p, start):
        for r in range(out.shape[0]):
            out[r, p, :, start : start + part.shape[1]] = part[r * rows : (r + 1) * rows]

    rests = []
    for p in range(3):
        t = own[:, width:] if p == 2 else own[:, :width]
        first, second, rest = pieces(held, away, p)
        store(mm(t, first, NT).astype(B), p, 0)
        store(mm(t, second, NT).astype(B), p, main)
        rests.append(rest)
    cut = rests[0].shape[0]
    part = mm(own[:, :width], jnp.concatenate(rests[:2], 0), NT).astype(B)
    store(part[:, :cut], 0, 2 * main)
    store(part[:, cut:], 1, 2 * main)
    store(mm(own[:, width:], rests[2], NT).astype(B), 2, 2 * main)


def back_kernel(got, spread):
    gate, up, back = (sum(got[r, i].astype(F) for r in range(got.shape[0])) for i in range(3))
    sig = jax.nn.sigmoid(gate)
    active = gate * sig
    hidden = (active * up).astype(B)
    grad_gate = (back * up * sig * (1.0 + gate * (1.0 - sig))).astype(B)
    grad_up = (back * active).astype(B)
    for r in range(spread.shape[0]):
        spread[r, 0] = grad_gate
        spread[r, 1] = grad_up
        spread[r, 2] = hidden


def plane(grads, p):
    ranks, _, rows, hid = grads.shape
    return grads[:, p].reshape(ranks * rows, hid)


def input_kernel(grads, held, away, out):
    g = jnp.concatenate([plane(grads, 0), plane(grads, 1)], 1)
    w = jnp.concatenate([piece for p in range(2) for piece in pieces(held, away, p)], 0)
    out[...] = mm(g, w, NN).astype(B)


def send_kernel(grads, own, out):
    cut = (out.shape[1] - own.shape[1]) // 3
    for p in range(3):
        out[:, p * cut : (p + 1) * cut] = plane(grads, p)[:, cut - 128 :]
    out[:, 3 * cut :] = own[...]


def own_weight_kernel(grads, own, out):
    hid, width = out.shape[1:]
    main = main_of(hid)
    for p in range(3):
        t = own[:, width:] if p == 2 else own[:, :width]
        g = plane(grads, p)
        out[p, :main] = mm(g[:, :main], t, TN)
        out[p, main:] = mm(g[:, 2 * main :], t, TN)[: hid - main]


def weight_kernel(first, got, *outs):
    hid, width = first.shape[1:]
    main = main_of(hid)
    cut = main + 128
    other = 3 * cut
    for p, out in enumerate(outs):
        t = got[:, other + width :] if p == 2 else got[:, other : other + width]
        g = got[:, p * cut : (p + 1) * cut]
        out[:main] = (first[p, :main] + mm(g[:, :main], t, TN)).astype(B)
        out[main:] = (first[p, main:] + mm(g[:, main:], t, TN)[hid - main :]).astype(B)


def spread_over(x, axes):
    return lax.all_to_all(x, axes, split_axis=0, concat_axis=0, tiled=True)


PATH = [(0, 0), (0, 1), (0, 2), (0, 3), (1, 3), (1, 2), (1, 1), (2, 1)]
PATH += [(2, 2), (2, 3), (3, 3), (3, 2), (3, 1), (3, 0), (2, 0), (1, 0)]


def rows_of(shape):
    ids = np.arange(int(np.prod(shape))).reshape(shape)
    return [[int(ids[x, y, z, c]) for x, y in (PATH, PATH[::-1])[c]] for z in range(shape[2]) for c in range(2)]


def over_rows(v, shape):
    return lax.all_to_all(v, ALL, split_axis=0, concat_axis=0, tiled=True, axis_index_groups=rows_of(shape))


def swapped(x):
    return lax.ppermute(x, "c", SWAP)


def per_device(shape, tokens, out_grad, w_gate, w_up, w_down):
    hid, width = w_down.shape
    depth = lax.axis_size("z")
    weights = [pltpu.with_memory_space_constraint(w, pltpu.HBM) for w in (w_gate.T, w_up.T, w_down)]
    held = call(load_kernel, ((3, hid, width), B), weights=weights, scratch=[pltpu.SemaphoreType.DMA((3,))])
    away = swapped(held)
    mine, held = lax.optimization_barrier((jnp.concatenate([tokens, out_grad], 1), held))
    own = lax.all_gather(mine, "z", axis=0, tiled=True)
    half = own.shape[0]
    ranks = SIDE * SIDE

    sizes = (ranks, 3, half // ranks, 2 * hid)
    parts = call(parts_kernel, (sizes, B), own, held, away)
    spread = call(back_kernel, (sizes, B), over_rows(parts, shape))
    grads = over_rows(spread, shape)

    part = call(input_kernel, ((half, width), B), grads, held, away)
    part, grads, own = lax.optimization_barrier((part.reshape(depth, half // depth, width), grads, own))
    part = spread_over(part, "z")
    got = swapped(call(send_kernel, ((half, 3 * (main_of(hid) + 128) + 2 * width), B), grads, own, cost=256))
    first = call(own_weight_kernel, ((3, hid, width), F), grads, own, cost=1 << 35)
    grad_gate_w, grad_up_w, grad_down_w = call(
        weight_kernel, [((hid, width), B)] * 3, first, got, cost=256
    )
    part, grad_gate_w, grad_up_w, grad_down_w = lax.optimization_barrier(
        (part, grad_gate_w, grad_up_w, grad_down_w)
    )
    grad_input = jnp.sum(part.astype(F), 0).astype(B)
    return (grad_input, grad_gate_w.T, grad_up_w.T, grad_down_w)


def solution(mesh):
    shape = (SIDE, SIDE, mesh.devices.shape[1] // 2, 2)
    mesh = Mesh(mesh.devices.reshape(shape), ALL)
    col = ("z", "c")
    placed = (P(col, ROW), P(col, ROW), P(ROW, col), P(ROW, col), P(col, ROW))
    return jax.shard_map(
        functools.partial(per_device, shape),
        mesh=mesh,
        in_specs=placed,
        out_specs=(P(col, ROW), P(ROW, col), P(ROW, col), P(col, ROW)),
        check_vma=False,
    )
```
